32 devices in a mesh: dp: 2 (over x), feat: 16 (over z, y, core).
Axes of the slice: x: 2, y: 2, z: 4, core: 2. Of those that a mesh axis runs over, the one named last changes fastest.
Arguments:
- feature_slab: float32 [1024, 28672], P('dp', 'feat'), may hold values from -200 to 200, as said below
- basis_start: float32 [28672, 256], P('feat'), may hold values from -0.03125 to 0.03125
Outputs:
- basis_out: float32 [28672, 256], P('feat')
The draws below stay inside these ranges and needn't reach their ends.
Inputs may be any that keep to these rules, and one draw needn't show every extreme that they name: `feature_slab`: Real-valued entries; column scales differ over features and row scales over rows.
All inputs are finite; a program needn't handle non-finite values.
Results may differ from the reference program's by a relative error of at most 0.0015.
Values sent between devices are 32-bit elements; how exact they have to be, the bound alone decides.
A program may use at most 64 MiB of HBM per device.

```python
import math
import jax
import jax.numpy as jnp
from jax import lax

FF = 28672
RANK = 256
ROWS = 512
ROUNDS = 1
NS_STEPS = 5
TOTAL_ROWS = 1024
N_DP = 2


def draw_feature_slab(key, part):
    key_cols, key_rows, key_vals = jax.random.split(jax.random.fold_in(key, 11), 3)
    column_scale = jnp.exp(jax.random.uniform(key_cols, (FF,), jnp.float32, 0.0, math.log(10.0)))
    column_scale = column_scale * jnp.exp(jnp.linspace(0.0, math.log(3.0), FF, dtype=jnp.float32))
    values = jax.random.normal(key_vals, (TOTAL_ROWS, FF), jnp.float32)
    row_scale = jnp.exp(jax.random.uniform(key_rows, (TOTAL_ROWS, 1), jnp.float32, 0.0, math.log(3.0)))
    return jnp.clip(values * row_scale * column_scale[None, :] / 8.0, -200.0, 200.0)


def steps_of(own_key, shape, cuts, least, high):
    factor_of = 1.0
    for dim, parts in cuts:
        heights = jax.random.uniform(jax.random.fold_in(jax.random.fold_in(own_key, 6), dim), (parts,), jnp.float32, least / len(cuts), high / len(cuts))
        factor_of = factor_of * jnp.repeat(jnp.exp(heights), shape[dim] // parts).reshape((-1,) + (1,) * (len(shape) - 1 - dim))
    return factor_of


def scatter_about(key, extent, deviation, reach, cuts=(), held_as=jnp.bfloat16):
    entries = jax.random.normal(key, extent, jnp.float32) * deviation
    if len(cuts) > 0:
        entries = steps_of(key, extent, cuts, -0.22, 0.18) * entries
    return jnp.clip(entries, min=-reach, max=reach).astype(held_as)


def setup_inputs(seed: int = 0) -> dict:
    key_of = jax.random.split(jax.random.key(seed), 3)
    feature_slab = draw_feature_slab(jax.random.fold_in(key_of[2], 71), 0)
    basis_start = scatter_about(key_of[1], (FF, RANK), FF ** -0.5, 0.03125, ((0, 16),), jnp.float32)
    return dict(feature_slab=feature_slab, basis_start=basis_start)


coef_first = 3.4445
coef_second = -4.775
coef_third = 2.0315

def plain_dot(left, right):
    return jnp.dot(left.astype(jnp.float32), right.astype(jnp.float32), precision=lax.Precision.HIGHEST, preferred_element_type=jnp.float32)

def newton_schulz(matrix):
    polar_iter = matrix / jnp.sqrt(jnp.sum(matrix * matrix) + 1e-12)
    for step_index in range(NS_STEPS):
        square_part = plain_dot(polar_iter, polar_iter.T)
        mixed_part = coef_second * square_part + coef_third * plain_dot(square_part, square_part)
        polar_iter = coef_first * polar_iter + plain_dot(mixed_part, polar_iter)
    return polar_iter

def group_round(group_slab, basis):
    projected = plain_dot(group_slab, basis)
    power_image = plain_dot(group_slab.T, projected)
    gram_matrix = plain_dot(power_image.T, power_image)
    lower_factor = jnp.linalg.cholesky(gram_matrix)
    identity = jnp.eye(RANK, dtype=basis.dtype)
    inverse = jax.scipy.linalg.solve_triangular(lower_factor, identity, lower=True)
    orthonormal = plain_dot(power_image, inverse.T)
    correlation = plain_dot(basis.T, orthonormal)
    return plain_dot(orthonormal, newton_schulz(correlation.T))

def reference(feature_slab, basis_start):
    basis = basis_start
    for round_index in range(ROUNDS):
        summed = jnp.zeros_like(basis)
        for group_index in range(N_DP):
            group_slab = feature_slab[group_index * ROWS:(group_index + 1) * ROWS]
            summed = summed + group_round(group_slab, basis)
        basis = summed / N_DP
    return basis * math.sqrt(FF)
```

```python
import functools
import math

import jax
import jax.numpy as jnp
from jax import lax
from jax.experimental import pallas as pl
from jax.experimental.pallas import tpu as pltpu
from jax.sharding import PartitionSpec as P

NS_STEPS = 5

coef_first = 3.4445
coef_second = -4.775
coef_third = 2.0315

MESH = pl.DeviceIdType.MESH
NN = (((1,), (0,)), ((), ()))
NT = (((1,), (1,)), ((), ()))
TN = (((0,), (0,)), ((), ()))


def dot6(left, right, dims=NN):
    return lax.dot_general(
        left, right, dims, precision=lax.Precision.HIGHEST, preferred_element_type=jnp.float32
    )


def halves(value):
    high = value.astype(jnp.bfloat16)
    low = (value - high.astype(jnp.float32)).astype(jnp.bfloat16)
    return high, low


def dot3(left, right, dims=NN):
    def dot(a, b):
        return lax.dot_general(a, b, dims, preferred_element_type=jnp.float32)

    return dot(left[0], right[0]) + (dot(left[0], right[1]) + dot(left[1], right[0]))


def radices(count):
    found = []
    while count > 1:
        radix = 2 if len(found) < 2 else 4
        if count % radix:
            radix = 2 if count % 2 == 0 else count
        found.append(radix)
        count //= radix
    return found


def stages_of(count):
    stride, out = 1, []
    for radix in radices(count):
        out.append((radix, stride))
        stride *= radix
    return out


def inverse_factor(block):
    size = block.shape[0]
    lane = lax.broadcasted_iota(jnp.int32, (1, size), 1)
    step = size // 4
    done = []
    top = 0
    for k in range(size):
        if k and k % step == 0:
            done.append(block[:step])
            block = block[step:]
            top = k
        row_id = lax.broadcasted_iota(jnp.int32, block.shape, 0) + top
        lane_id = lax.broadcasted_iota(jnp.int32, block.shape, 1)
        row = block[k - top : k - top + 1, :]
        scale = 1.0 / row[:, k : k + 1]
        row = jnp.where(lane == k, 1.0, row) * scale
        column = jnp.where(row_id[:, :1] > k, block[:, k : k + 1], 0.0)
        block = jnp.where((lane_id == k) & (row_id > k), 0.0, block) - column * row
    done.append(block)
    block = jnp.concatenate(done, axis=0)
    row_id = lax.broadcasted_iota(jnp.int32, block.shape, 0)
    lane_id = lax.broadcasted_iota(jnp.int32, block.shape, 1)
    pivots = jnp.sum(jnp.where(row_id == lane_id, block, 0.0), axis=1, keepdims=True)
    unit = jnp.where(row_id > lane_id, block, jnp.where(row_id == lane_id, 1.0, 0.0))
    return unit * (1.0 / jnp.sqrt(pivots))


def all_reduce(buf, total, slots, sems, stages, me):
    send1, recv1, send2, recv2 = sems
    rows = buf.shape[0]
    at, length, sem = 0, rows, 0
    places = []
    for (radix, stride), slot in zip(stages, slots):
        digit = lax.rem(lax.div(me, stride), radix)
        length //= radix
        copies = []
        for o in range(1, radix):
            other = lax.rem(digit + o, radix)
            copy = pltpu.make_async_remote_copy(
                src_ref=buf.at[pl.ds(pl.multiple_of(at + other * length, 8), length)],
                dst_ref=slot.at[o - 1],
                send_sem=send1.at[sem],
                recv_sem=recv1.at[sem],
                device_id={"feat": me + (other - digit) * stride},
                device_id_type=MESH,
            )
            copy.start()
            copies.append(copy)
            sem += 1
        at = pl.multiple_of(at + digit * length, 8)
        places.append((radix, stride, digit, at, length))
        for copy in copies:
            copy.wait()
        mine = buf[pl.ds(at, length)]
        for o in range(1, radix):
            mine = mine + slot[o - 1]
        if stride * radix == math.prod(r for r, _ in stages):
            total[pl.ds(at, length)] = mine
        else:
            buf[pl.ds(at, length)] = mine
    sem = 0
    for radix, stride, digit, at, length in reversed(places):
        copies = []
        for o in range(1, radix):
            other = lax.rem(digit + o, radix)
            copy = pltpu.make_async_remote_copy(
                src_ref=total.at[pl.ds(at, length)],
                dst_ref=total.at[pl.ds(at, length)],
                send_sem=send2.at[sem],
                recv_sem=recv2.at[sem],
                device_id={"feat": me + (other - digit) * stride},
                device_id_type=MESH,
            )
            copy.start()
            copies.append(copy)
            sem += 1
        for copy in copies:
            copy.wait()


def kernel(cfg, a_ref, b_ref, o_ref, *refs):
    stages, groups, chunks, width, scale_out = cfg
    n = len(stages)
    s_buf, proj, g_buf, g_sum, pit, pit_in, m_buf, m_in = refs[:8]
    s_slots, g_slots = refs[8 : 8 + n], refs[8 + n : 8 + 2 * n]
    s_sems, g_sems = refs[8 + 2 * n : 12 + 2 * n], refs[12 + 2 * n : 16 + 2 * n]
    p_send, p_recv, m_send, m_recv = refs[16 + 2 * n : 20 + 2 * n]
    rank = b_ref.shape[1]
    half = rank // 2
    me = lax.axis_index("feat")
    group = lax.axis_index("dp")

    barrier = pltpu.get_barrier_semaphore()
    count = 0
    for radix, stride in stages:
        digit = lax.rem(lax.div(me, stride), radix)
        for o in range(1, radix):
            other = lax.rem(digit + o, radix)
            pl.semaphore_signal(
                barrier, inc=1, device_id={"feat": me + (other - digit) * stride}, device_id_type=MESH
            )
            count += 1
    for o in range(1, groups):
        pl.semaphore_signal(
            barrier, inc=1, device_id={"dp": lax.rem(group + o, groups)}, device_id_type=MESH
        )
        count += 1

    def columns(c):
        return pl.ds(pl.multiple_of(c * width, width), width) if chunks > 1 else pl.ds(0, width)

    s_buf[...] = jnp.zeros_like(s_buf)

    @pl.loop(0, chunks)
    def _(c):
        s_buf[...] += dot3(halves(a_ref[:, columns(c)]), halves(b_ref[columns(c), :]))

    pl.semaphore_wait(barrier, count)
    all_reduce(s_buf, proj, s_slots, s_sems, stages, me)

    def exchange(c, o):
        return pltpu.make_async_remote_copy(
            src_ref=pit.at[c],
            dst_ref=pit_in.at[o - 1, c],
            send_sem=p_send.at[o - 1, c],
            recv_sem=p_recv.at[o - 1, c],
            device_id={"dp": lax.rem(group + o, groups)},
            device_id_type=MESH,
        )

    projected = halves(proj[...].T)
    m_buf[...] = jnp.zeros_like(m_buf)

    @pl.loop(0, chunks)
    def _(c):
        image = dot3(projected, halves(a_ref[:, columns(c)]))
        pit[c] = image
        for o in range(1, groups):
            exchange(c, o).start()
        pair = halves(image)
        m_buf[...] += dot3(pair, pair, NT)

    g_buf[0:half] = m_buf[:half, :half]
    g_buf[half : 2 * half] = m_buf[:half, half:]
    g_buf[2 * half : 3 * half] = m_buf[half:, half:]
    if g_buf.shape[0] > 3 * half:
        g_buf[3 * half :] = jnp.zeros_like(g_buf[3 * half :])
    all_reduce(g_buf, g_sum, g_slots, g_sems, stages, me)

    first = inverse_factor(g_sum[0:half])
    upper = dot6(first, g_sum[half : 2 * half])
    last = inverse_factor(g_sum[2 * half : 3 * half] - dot6(upper, upper, TN))
    low = -dot6(last, dot6(upper, first, TN))
    inverse = jnp.concatenate(
        [
            jnp.concatenate([first, jnp.zeros_like(first)], axis=1),
            jnp.concatenate([low, last], axis=1),
        ],
        axis=0,
    )
    cross = dot6(proj[...], proj[...], TN)
    matrix = dot6(inverse, cross)
    polar = matrix / jnp.sqrt(jnp.sum(matrix * matrix, keepdims=True) + 1e-12)
    for _ in range(NS_STEPS):
        square = dot6(polar, polar, NT)
        mixed = coef_second * square + coef_third * dot6(square, square)
        polar = coef_first * polar + dot6(mixed, polar)
    m_buf[...] = dot6(inverse, polar, TN) * scale_out

    def share(o):
        return pltpu.make_async_remote_copy(
            src_ref=m_buf,
            dst_ref=m_in.at[o - 1],
            send_sem=m_send.at[o - 1],
            recv_sem=m_recv.at[o - 1],
            device_id={"dp": lax.rem(group + o, groups)},
            device_id_type=MESH,
        )

    for o in range(1, groups):
        share(o).start()
    own = halves(m_buf[...])

    @pl.loop(0, chunks)
    def _(c):
        o_ref[columns(c), :] = dot3(halves(pit[c].T), own)

    for o in range(1, groups):
        share(o).wait()
        theirs = halves(m_in[o - 1])

        @pl.loop(0, chunks)
        def _(c):
            exchange(c, o).wait()
            o_ref[columns(c), :] += dot3(halves(pit_in[o - 1, c].T), theirs)


def per_device(feature_slab, basis_start):
    feats, groups = lax.axis_size("feat"), lax.axis_size("dp")
    rows, features = feature_slab.shape
    rank = basis_start.shape[1]
    half = rank // 2
    width = 256 if features % 256 == 0 else features
    chunks = features // width
    stages = stages_of(feats)
    g_rows = -(-3 * half // (8 * feats)) * 8 * feats
    copies = sum(r - 1 for r, _ in stages)
    f32 = jnp.float32

    def slots(count, cols):
        out = []
        for radix, _ in stages:
            count //= radix
            out.append(pltpu.VMEM((radix - 1, count, cols), f32))
        return out

    scratch = [
        pltpu.VMEM((rows, rank), f32),
        pltpu.VMEM((rows, rank), f32),
        pltpu.VMEM((g_rows, half), f32),
        pltpu.VMEM((g_rows, half), f32),
        pltpu.VMEM((chunks, rank, width), f32),
        pltpu.VMEM((groups - 1, chunks, rank, width), f32),
        pltpu.VMEM((rank, rank), f32),
        pltpu.VMEM((groups - 1, rank, rank), f32),
        *slots(rows, rank),
        *slots(g_rows, half),
        *[pltpu.SemaphoreType.DMA((copies,)) for _ in range(8)],
        pltpu.SemaphoreType.DMA((groups - 1, chunks)),
        pltpu.SemaphoreType.DMA((groups - 1, chunks)),
        pltpu.SemaphoreType.DMA((groups - 1,)),
        pltpu.SemaphoreType.DMA((groups - 1,)),
    ]
    scale_out = math.sqrt(features * feats) / groups
    return pl.pallas_call(
        functools.partial(kernel, (stages, groups, chunks, width, scale_out)),
        out_shape=jax.ShapeDtypeStruct((features, rank), f32),
        in_specs=[pl.BlockSpec(memory_space=pltpu.VMEM)] * 2,
        out_specs=pl.BlockSpec(memory_space=pltpu.VMEM),
        scratch_shapes=scratch,
        compiler_params=pltpu.CompilerParams(
            collective_id=0, has_side_effects=True, vmem_limit_bytes=48 * 2**20
        ),
    )(feature_slab, basis_start)


def solution(mesh):
    placed = (P("dp", "feat"), P("feat", None))
    return jax.shard_map(
        per_device, mesh=mesh, in_specs=placed, out_specs=P("feat", None), check_vma=False
    )
```
